1024 devices in a mesh: dp: 64 (over z, x_hi, core), expert: 16 (over x_lo, y).
Axes of the slice: x: 4 (x_hi: 2, x_lo: 2; x = x_hi * 2 + x_lo), y: 8, z: 16, core: 2. Of those that a mesh axis runs over, the one named last changes fastest.
Arguments:
- teacher_in: bfloat16 [8192, 2048], P('dp'), may hold values from -6 to 6
- student_in: bfloat16 [8192, 2048], P('dp'), may hold values from -6 to 6
- teacher_route: int32 [8192, 1], P('dp'), may hold values from 0 to 31, as said below
- student_route: int32 [8192, 1], P('dp'), may hold values from 0 to 31, as said below
- teacher_w1: bfloat16 [64, 2048, 2048], P('dp', None, 'expert'), may hold values from -0.125 to 0.125
- teacher_w2: bfloat16 [64, 2048, 2048], P('dp', 'expert'), may hold values from -0.09375 to 0.09375
- student_w1: bfloat16 [64, 2048, 2048], P('dp', None, 'expert'), may hold values from -0.125 to 0.125
- student_w2: bfloat16 [64, 2048, 2048], P('dp', 'expert'), may hold values from -0.09375 to 0.09375
Outputs:
- grad_w1: bfloat16 [64, 2048, 2048], P('dp', None, 'expert')
- grad_w2: bfloat16 [64, 2048, 2048], P('dp', 'expert')
The draws below stay inside these ranges and needn't reach their ends.
Inputs may be any that keep to these rules, and one draw needn't show every extreme that they name: `teacher_route`: in each aligned block of 128 rows (the rows of one index of dp) no expert is named by more than 6 rows, and some expert exactly 6 times; every expert is named exactly 6 times in some block. `student_route`: in each aligned block of 128 rows (the rows of one index of dp) no expert is named by more than 6 rows, and some expert exactly 6 times; every expert is named exactly 6 times in some block.
All inputs are finite; a program needn't handle non-finite values.
Results may differ from the reference program's by a relative error of at most 0.015.
Values may be sent and summed in bfloat16 or wider, within the bound.
A program may use at most 64 MiB of HBM per device.

```python
import math
import jax
import jax.numpy as jnp
from jax import lax

D = 2048
FF = 4096
TOK_DEV = 128
EXPERTS = 32
CAP = 6
HID = 128
TOKENS = 8192
N_DP = 64


def route_table(key):
    key_offset, key_slots, key_rows = jax.random.split(key, 3)
    slot_total = EXPERTS * CAP
    offset = jax.random.randint(key_offset, (), 0, EXPERTS, dtype=jnp.int32)
    full_expert = (jnp.arange(N_DP, dtype=jnp.int32) + offset) % EXPERTS
    slot_iota = jnp.arange(slot_total, dtype=jnp.int32)
    slot_expert = slot_iota // CAP
    forced = slot_expert[None, :] == full_expert[:, None]
    raw_scores = jax.random.randint(key_slots, (N_DP, slot_total), 0, 2 ** 19, dtype=jnp.int32)
    scores = jnp.where(forced, -1 - slot_iota[None, :], raw_scores * slot_total + slot_iota[None, :])
    order = jnp.argsort(scores, axis=1, stable=True)[:, :TOK_DEV].astype(jnp.int32)
    chosen = order // CAP
    row_iota = jnp.arange(TOK_DEV, dtype=jnp.int32)
    row_scores = jax.random.randint(key_rows, (N_DP, TOK_DEV), 0, 2 ** 19, dtype=jnp.int32) * TOK_DEV + row_iota[None, :]
    shuffle = jnp.argsort(row_scores, axis=1, stable=True).astype(jnp.int32)
    mixed = jnp.take_along_axis(chosen, shuffle, axis=1)
    return mixed.reshape(TOKENS, 1).astype(jnp.int32)


def draw_teacher_route(key, part):
    key = jax.random.fold_in(key, 11)
    return route_table(key)


def draw_student_route(key, part):
    key = jax.random.fold_in(key, 23)
    return route_table(key)


def block_levels(stream_key, shape, shards, least, high):
    factor_of = 1.0
    for dim, shards_of in shards:
        heights = jax.random.uniform(jax.random.fold_in(jax.random.fold_in(stream_key, 6), dim), (shards_of,), jnp.float32, least / len(shards), high / len(shards))
        factor_of = factor_of * jnp.repeat(jnp.exp(heights), shape[dim] // shards_of).reshape((-1,) + (1,) * (len(shape) - 1 - dim))
    return factor_of


def gaussian(rng, shape, spread, limit, shards=(), held_as=jnp.bfloat16):
    loudness = block_levels(rng, shape, shards, -0.22, 0.18) if shards else 1.0
    array = jax.random.normal(rng, shape, jnp.float32) * spread * loudness
    return jnp.minimum(jnp.maximum(array, -limit), limit).astype(held_as)


def setup_inputs(seed: int = 0) -> dict:
    key_of = jax.random.split(jax.random.key(seed), 9)
    return {
        "teacher_in": gaussian(key_of[0], (TOKENS, D), 1.0, 6.0, ((0, 64),)),
        "student_in": gaussian(key_of[1], (TOKENS, D), 1.0, 6.0, ((0, 64),)),
        "teacher_route": draw_teacher_route(jax.random.fold_in(key_of[8], 71), 0),
        "student_route": draw_student_route(jax.random.fold_in(key_of[8], 71), 0),
        "teacher_w1": gaussian(key_of[4], (2 * EXPERTS, D, FF // 2), D ** -0.5, 0.125, ((0, 64), (2, 16))),
        "teacher_w2": gaussian(key_of[5], (2 * EXPERTS, FF // 2, D), FF ** -0.5, 0.09375, ((0, 64), (1, 16))),
        "student_w1": gaussian(key_of[6], (2 * EXPERTS, D, FF // 2), D ** -0.5, 0.125, ((0, 64), (2, 16))),
        "student_w2": gaussian(key_of[7], (2 * EXPERTS, FF // 2, D), FF ** -0.5, 0.09375, ((0, 64), (1, 16))),
    }


root_coef = math.sqrt(2.0 / math.pi)
cubic_coef = 0.044715

def gelu_tanh(pre_act):
    inner_arg = root_coef * (pre_act + cubic_coef * pre_act * pre_act * pre_act)
    return 0.5 * pre_act * (1.0 + jnp.tanh(inner_arg))

def gelu_slope(pre_act):
    tangent = jnp.tanh(root_coef * (pre_act + cubic_coef * pre_act * pre_act * pre_act))
    return 0.5 * (1.0 + tangent) + 0.5 * pre_act * (1.0 - tangent * tangent) * root_coef * (1.0 + 3.0 * cubic_coef * pre_act * pre_act)

def slot_positions(routes):
    choose = routes[:, 0].astype(jnp.int32)
    onehot = (choose[:, None] == jnp.arange(EXPERTS, dtype=jnp.int32)[None, :]).astype(jnp.int32)
    blocked = onehot.reshape(N_DP, TOK_DEV, EXPERTS)
    rank_table = jnp.cumsum(blocked, axis=1) - 1
    position = lax.optimization_barrier(jnp.sum(blocked * rank_table, axis=2)).reshape(TOKENS).astype(jnp.int32)
    block_id = (jnp.arange(TOKENS, dtype=jnp.int32) // TOK_DEV).astype(jnp.int32)
    return (choose, block_id, position)

def to_slots(values, route_info):
    choose, block_id, position = route_info
    empty = jnp.zeros((EXPERTS, N_DP, CAP, D), values.dtype)
    return empty.at[choose, block_id, position].set(values)

def from_slots(slots, route_info):
    choose, block_id, position = route_info
    return slots[choose, block_id, position]

def join_first(w1_pair):
    return jnp.concatenate([w1_pair[0], w1_pair[1]], axis=1)

def expert_output(x_rows, w1_pair, w2_full):
    pre_act = jnp.dot(x_rows, join_first(w1_pair), preferred_element_type=jnp.float32)
    hidden = gelu_tanh(pre_act).astype(jnp.bfloat16)
    group_count = FF // HID
    parts = jnp.einsum('sgi,gid->sgd', hidden.reshape(-1, group_count, HID).astype(jnp.float32), w2_full.reshape(group_count, HID, D).astype(jnp.float32))
    rounded = lax.optimization_barrier(parts.astype(jnp.bfloat16))
    return lax.optimization_barrier(jnp.sum(rounded.astype(jnp.float32), axis=1))

def forward_expert(inputs):
    teacher_slots, student_slots, w1_teacher, w2_teacher, w1_student, w2_student = inputs
    teacher_out = expert_output(teacher_slots.reshape(-1, D), w1_teacher, w2_teacher)
    student_out = expert_output(student_slots.reshape(-1, D), w1_student, w2_student)
    return (teacher_out, student_out)

def backward_expert(inputs):
    student_slots, grad_slots, w1_student, w2_student = inputs
    x_rows = student_slots.reshape(-1, D)
    up_rows = grad_slots.reshape(-1, D)
    pre_act = jnp.dot(x_rows, join_first(w1_student), preferred_element_type=jnp.float32)
    hidden = gelu_tanh(pre_act).astype(jnp.bfloat16)
    hidden_grad = jnp.dot(up_rows, w2_student.T, preferred_element_type=jnp.float32)
    pre_grad = (hidden_grad * gelu_slope(pre_act)).astype(jnp.bfloat16)
    grad_second = jnp.dot(hidden.T, up_rows, preferred_element_type=jnp.float32).astype(jnp.bfloat16)
    grad_first = jnp.dot(x_rows.T, pre_grad, preferred_element_type=jnp.float32).astype(jnp.bfloat16)
    grad_first = grad_first.reshape(D, 2, FF // 2).transpose(1, 0, 2)
    return (grad_first, grad_second)

def reference(teacher_in, student_in, teacher_route, student_route, teacher_w1, teacher_w2, student_w1, student_w2):
    teacher_info = slot_positions(teacher_route)
    student_info = slot_positions(student_route)
    w1_teacher = teacher_w1.reshape(EXPERTS, 2, D, FF // 2)
    w2_teacher = teacher_w2.reshape(EXPERTS, FF, D)
    w1_student = student_w1.reshape(EXPERTS, 2, D, FF // 2)
    w2_student = student_w2.reshape(EXPERTS, FF, D)
    teacher_slots = to_slots(teacher_in, teacher_info)
    student_slots = to_slots(student_in, student_info)
    teacher_sums, student_sums = lax.map(forward_expert, (teacher_slots, student_slots, w1_teacher, w2_teacher, w1_student, w2_student))
    teacher_out = from_slots(teacher_sums.reshape(EXPERTS, N_DP, CAP, D), teacher_info)
    student_out = from_slots(student_sums.reshape(EXPERTS, N_DP, CAP, D), student_info)
    upstream = ((student_out - teacher_out) * (1.0 / math.sqrt(TOK_DEV))).astype(jnp.bfloat16)
    grad_slots = to_slots(upstream, student_info)
    grad_first, grad_second = lax.map(backward_expert, (student_slots, grad_slots, w1_student, w2_student))
    grad_w1 = grad_first.reshape(2 * EXPERTS, D, FF // 2)
    grad_w2 = grad_second.reshape(2 * EXPERTS, FF // 2, D)
    return (grad_w1, grad_w2)
```

```python
import functools
import math

import jax
import jax.numpy as jnp
from jax import lax
from jax.experimental import pallas as pl
from jax.experimental.pallas import tpu as pltpu
from jax.sharding import PartitionSpec as P

root_coef = math.sqrt(2.0 / math.pi)
cubic_coef = 0.044715
MESH = pl.DeviceIdType.MESH
F32 = jnp.float32
BF16 = jnp.bfloat16
CAP = 6
PAD = 16
X = 2


def gelu_tanh(pre_act):
    inner_arg = root_coef * (pre_act + cubic_coef * pre_act * pre_act * pre_act)
    return 0.5 * pre_act * (1.0 + jnp.tanh(inner_arg))


def gelu_slope(pre_act):
    tangent = jnp.tanh(root_coef * (pre_act + cubic_coef * pre_act * pre_act * pre_act))
    return 0.5 * (1.0 + tangent) + 0.5 * pre_act * (1.0 - tangent * tangent) * root_coef * (
        1.0 + 3.0 * cubic_coef * pre_act * pre_act
    )


def dot(a, b, ca, cb):
    return lax.dot_general(a, b, (((ca,), (cb,)), ((), ())), preferred_element_type=F32)


def iota(shape, dim):
    return lax.broadcasted_iota(jnp.int32, shape, dim)


def slot_rows(route):
    rows = route.shape[0]
    member = (route == iota((rows, 128), 1)).astype(F32)
    earlier = (iota((rows, rows), 0) >= iota((rows, rows), 1)).astype(F32)
    rank = dot(earlier.astype(BF16), member.astype(BF16), 1, 0)
    position = jnp.sum(member * rank, axis=1, keepdims=True) - 1.0
    return route * PAD + position.astype(jnp.int32)


def kernel(
    experts,
    Y,
    xt_hbm,
    xs_hbm,
    rt_ref,
    rs_ref,
    w1t_hbm,
    w2t_hbm,
    w1s_hbm,
    w2s_hbm,
    g1_ref,
    g2_ref,
    xcol,
    w1t,
    w2t,
    w1s,
    w2s,
    place,
    gapper,
    out1,
    in1,
    out2,
    in2,
    out3,
    in3,
    xt,
    xs,
    gr,
    pt,
    ps,
    lt,
    ls,
    landt,
    lands,
    staget,
    stages,
    finals,
    xsend,
    xland,
    pre_ref,
    hid_ref,
    load_sem,
    a_send,
    a_recv,
    g_send,
    g_recv,
    r_send,
    r_recv,
):
    H = Y // 2
    tokens, C = xcol.shape[1], xcol.shape[2]
    R = experts * CAP
    per = min(8, experts)
    groups = experts // per
    me = lax.axis_index("dp")
    mine = lax.axis_index("expert")
    k, c = me // 2, me % 2
    x, y = mine // Y, mine % Y
    up_y, down_y = (y + 1) % Y, (y + Y - 1) % Y

    here = (me, mine)
    sibling = (k * 2 + 1 - c, mine)
    across = (me, (1 - x) * Y + y)
    above = (me, x * Y + up_y)
    below = (me, x * Y + down_y)

    def remote(src, dst, send, recv, device):
        return pltpu.make_async_remote_copy(
            src_ref=src, dst_ref=dst, send_sem=send, recv_sem=recv, device_id=device, device_id_type=MESH
        )

    barrier = pltpu.get_barrier_semaphore()

    def greet(j, carry):
        pl.semaphore_signal(
            barrier, inc=1, device_id=(((k + j) % experts) * 2 + c, mine), device_id_type=MESH
        )
        return carry

    lax.fori_loop(1, experts, greet, 0)
    for device in (sibling, across, above, below):
        pl.semaphore_signal(barrier, inc=1, device_id=device, device_id_type=MESH)

    columns = pl.ds(pl.multiple_of(mine * C, C), C)
    loads = [
        pltpu.make_async_copy(xt_hbm.at[:, columns], xcol.at[0], load_sem.at[0]),
        pltpu.make_async_copy(xs_hbm.at[:, columns], xcol.at[1], load_sem.at[1]),
        pltpu.make_async_copy(w1t_hbm, w1t, load_sem.at[2]),
        pltpu.make_async_copy(w2t_hbm, w2t, load_sem.at[3]),
        pltpu.make_async_copy(w1s_hbm, w1s, load_sem.at[4]),
        pltpu.make_async_copy(w2s_hbm, w2s, load_sem.at[5]),
    ]
    for load in loads:
        load.start()

    lanes = iota((tokens, experts * PAD), 1)
    from_t = (slot_rows(rt_ref[...]) == lanes).astype(F32)
    from_s = (slot_rows(rs_ref[...]) + CAP == lanes).astype(F32)
    gapper[...] = (from_s - from_t).astype(BF16)
    place[0] = from_t.astype(BF16)
    place[1] = from_s.astype(BF16)

    half = per * CAP
    col = iota((2 * half, per * PAD), 1)
    block, lane = col // PAD, col % PAD
    target = jnp.where(
        lane < CAP,
        block * CAP + lane,
        jnp.where(lane < 2 * CAP, half + block * CAP + lane - CAP, -1),
    )
    pack = (iota((2 * half, per * PAD), 0) == target).astype(F32).astype(BF16)

    loads[0].wait()
    loads[1].wait()
    both = jnp.concatenate([place[0], place[1]], axis=0)
    values = jnp.concatenate([xcol[0], xcol[1]], axis=0)
    out1[...] = dot(both, values, 0, 0).astype(BF16).reshape(experts, PAD, C)

    pl.semaphore_wait(barrier, experts - 1 + 4)

    def exchange_start(n, src, dst):
        def send(j, carry):
            other = (k + j) % experts
            remote(src.at[other], dst.at[k], a_send.at[n], a_recv.at[n], (other * 2 + c, mine)).start()
            return carry

        lax.fori_loop(1, experts, send, 0)
        dst[k] = src[k]

    def exchange_wait(n, dst):
        if experts > 1:
            many = dst.at[pl.ds(0, experts - 1)]
            pltpu.make_async_copy(many, many, a_recv.at[n]).wait()

    def exchange_sent(n, src):
        if experts > 1:
            many = src.at[pl.ds(0, experts - 1)]
            pltpu.make_async_copy(many, many, a_send.at[n]).wait()

    started = []

    def go(copy):
        copy.start()
        started.append(copy)
        return copy

    lower, upper = pl.ds(0, R // 2), pl.ds(R // 2, R // 2)

    class Gather:
        def __init__(self, n, buf):
            self.n, self.buf, self.siblings = n, buf, 0
            own = buf.at[c, y, x]
            self.cross = go(remote(own, own, g_send.at[n, 0], g_recv.at[n, 0], across))
            self.ring = {}

        def to_sibling(self, part):
            i = 1 + 2 * H + self.siblings
            self.siblings += 1
            go(remote(part, part, g_send.at[self.n, i], g_recv.at[self.n, 1 + 2 * H], sibling))

        def send(self, way, s):
            from_y = (y + Y - (s - 1)) % Y if way == 0 else (y + s - 1) % Y
            part = self.buf.at[self_c, from_y]
            if s == H:
                part = part.at[:, lower if way == 0 else upper]
            i = 1 + way * H + s - 1
            self.ring[way, s] = go(
                remote(part, part, g_send.at[self.n, i], g_recv.at[self.n, i], above if way == 0 else below)
            )

        def step(self, s):
            if s == 0:
                self.cross.wait_recv()
                self.send(0, 1)
                self.send(1, 1)
                self.to_sibling(self.buf.at[c, y])
                return
            for way in (0, 1):
                self.ring[way, s].wait_recv()
                if s < H:
                    self.send(way, s + 1)
                    from_y = (y + Y - s) % Y if way == 0 else (y + s) % Y
                    self.to_sibling(self.buf.at[c, from_y])
            if s == H:
                self.to_sibling(self.buf.at[c, (y + H) % Y])

        def finish(self):
            whole = self.buf.at[1 - c]
            pltpu.make_async_copy(whole, whole, g_recv.at[self.n, 1 + 2 * H]).wait()

    self_c = c

    def pack_rows(src, first, dsts):
        for g in range(groups):
            rows = dot(pack[first:], src[pl.ds(g * per, per)].reshape(per * PAD, C), 1, 0).astype(BF16)
            for i, dst in enumerate(dsts):
                dst[c, y, x, pl.ds(g * half, half)] = rows[i * half : (i + 1) * half]

    exchange_start(0, out1, in1)
    exchange_wait(0, in1)
    pack_rows(in1, 0, (xt, xs))

    gathers = [Gather(0, xt), Gather(1, xs)]
    for s in range(H + 1):
        for gather in gathers:
            gather.step(s)

    def pair_cols(ref, i):
        return jnp.concatenate([ref[:, i, 0].reshape(2 * R, C), ref[:, i, 1].reshape(2 * R, C)], axis=1)

    def w1_rows(ref, i):
        first = pl.ds(pl.multiple_of(i * C, C), C)
        second = pl.ds(pl.multiple_of((Y + i) * C, C), C)
        return first, second

    def forward(buf, w1, w2, part, keep):
        def first(i, total):
            a, b = w1_rows(w1, i)
            return total + dot(pair_cols(buf, i), jnp.concatenate([w1[a], w1[b]], axis=0), 1, 0)

        pre = lax.fori_loop(0, Y, first, jnp.zeros((2 * R, w1.shape[1]), F32))
        hidden = gelu_tanh(pre).astype(BF16)
        if keep:
            pre_ref[...] = pre
        hid_ref[...] = hidden

        def second(i, carry):
            a, b = w1_rows(w1, i)
            out = dot(hid_ref[...], jnp.concatenate([w2[:, a], w2[:, b]], axis=1), 1, 0).astype(BF16)
            part[:, i, 0] = out[:, :C].reshape(2, R, C)
            part[:, i, 1] = out[:, C:].reshape(2, R, C)
            return carry

        lax.fori_loop(0, Y, second, 0)

    class Scatter:
        def __init__(self, n, part, land, ring, stage):
            self.n, self.part, self.land, self.ring, self.stage = n, part, land, ring, stage
            self.sib = go(remote(part.at[1 - c], land, r_send.at[n, 0], r_recv.at[n, 0], sibling))
            self.copies = {}

        def own(self, i):
            return self.part[c, i].astype(F32) + self.land[i].astype(F32)

        def send(self, way, s):
            dst, src = self.ring.at[way, s - 1], self.stage.at[way, s - 1]
            if s == 1:
                rows = lower if way == 0 else upper
                dst, src = dst.at[:, rows], src.at[:, rows]
            i = 1 + way * H + s - 1
            self.copies[way, s] = go(
                remote(src, dst, r_send.at[self.n, i], r_recv.at[self.n, i], above if way == 0 else below)
            )

        def step(self, s):
            if s == 1:
                self.sib.wait_recv()
                value = self.own((y + H) % Y).astype(BF16)
                self.stage[0, 0, :, : R // 2] = value[:, : R // 2]
                self.stage[1, 0, :, R // 2 :] = value[:, R // 2 :]
                self.send(0, 1)
                self.send(1, 1)
                return
            away = H + 1 - s
            for way in (0, 1):
                own = self.own((y + away) % Y if way == 0 else (y + Y - away) % Y)
                self.copies[way, s - 1].wait_recv()
                if s == 2:
                    if way == 0:
                        top = own[:, : R // 2] + self.ring[0, 0, :, : R // 2].astype(F32)
                        self.stage[0, 1, :, : R // 2] = top.astype(BF16)
                        self.stage[0, 1, :, R // 2 :] = own[:, R // 2 :].astype(BF16)
                    else:
                        low = own[:, R // 2 :] + self.ring[1, 0, :, R // 2 :].astype(F32)
                        self.stage[1, 1, :, : R // 2] = own[:, : R // 2].astype(BF16)
                        self.stage[1, 1, :, R // 2 :] = low.astype(BF16)
                else:
                    total = own + self.ring[way, s - 2].astype(F32)
                    self.stage[way, s - 1] = total.astype(BF16)
                self.send(way, s)

        def last(self):
            total = self.own(y)
            for way in (0, 1):
                self.copies[way, H].wait_recv()
                total = total + self.ring[way, H - 1].astype(F32)
            finals[self.n] = total
            xsend[self.n] = finals[self.n, 1 - x].astype(BF16)
            i = 1 + 2 * H
            self.cross = go(
                remote(xsend.at[self.n], xland.at[self.n], r_send.at[self.n, i], r_recv.at[self.n, i], across)
            )

        def result(self):
            self.cross.wait_recv()
            return (finals[self.n, x] + xland[self.n].astype(F32)).astype(BF16)

    gathers[0].finish()
    loads[2].wait()
    loads[3].wait()
    forward(xt, w1t, w2t, pt, False)
    scatters = [Scatter(0, pt, lt, landt, staget)]
    gathers[1].finish()
    loads[4].wait()
    loads[5].wait()
    forward(xs, w1s, w2s, ps, True)
    scatters.append(Scatter(1, ps, ls, lands, stages))
    for s in range(1, H + 1):
        for scatter in scatters:
            scatter.step(s)
    for scatter in scatters:
        scatter.last()
    sum_t = scatters[0].result()
    sum_s = scatters[1].result()
    for g in range(groups):
        rows = slice(g * half, (g + 1) * half)
        spread = dot(pack, jnp.concatenate([sum_t[rows], sum_s[rows]], axis=0), 0, 0)
        out2[pl.ds(g * per, per)] = spread.astype(BF16).reshape(per, PAD, C)
    exchange_start(1, out2, in2)
    exchange_wait(1, in2)

    gap = dot(gapper[...], in2[...].reshape(experts * PAD, C), 1, 0)
    upstream = (gap * (1.0 / math.sqrt(tokens))).astype(BF16)
    out3[...] = dot(place[1], upstream, 0, 0).astype(BF16).reshape(experts, PAD, C)
    exchange_start(2, out3, in3)
    exchange_wait(2, in3)
    pack_rows(in3, half, (gr,))
    gather = Gather(2, gr)
    for s in range(H + 1):
        gather.step(s)
    gather.finish()

    def back_hidden(i, total):
        a, b = w1_rows(w2s, i)
        cols = pair_cols(gr, i)
        second = dot(hid_ref[...], cols, 0, 0).astype(BF16)
        g2_ref[:, a] = second[:, :C]
        g2_ref[:, b] = second[:, C:]
        return total + dot(cols, jnp.concatenate([w2s[:, a], w2s[:, b]], axis=1), 1, 1)

    hidden_grad = lax.fori_loop(0, Y, back_hidden, jnp.zeros(pre_ref.shape, F32))
    pre_grad = (hidden_grad * gelu_slope(pre_ref[...])).astype(BF16)

    def back_first(i, carry):
        a, b = w1_rows(w1s, i)
        first = dot(pair_cols(xs, i), pre_grad, 0, 0).astype(BF16)
        g1_ref[a] = first[:C]
        g1_ref[b] = first[C:]
        return carry

    lax.fori_loop(0, Y, back_first, 0)

    for copy in started:
        copy.wait_send()
    for n, src in ((0, out1), (1, out2), (2, out3)):
        exchange_sent(n, src)


def on_device(teacher_in, student_in, teacher_route, student_route, w1t, w2t, w1s, w2s):
    experts = lax.axis_size("dp") // 2
    spots = lax.axis_size("expert")
    Y = spots // X
    H = Y // 2
    tokens, width = teacher_in.shape
    C = width // spots
    hid = w1t.shape[2]
    R = experts * CAP
    vmem, dma = pltpu.VMEM, pltpu.SemaphoreType.DMA
    any_spec, vmem_spec = pl.BlockSpec(memory_space=pl.ANY), pl.BlockSpec(memory_space=vmem)
    message = vmem((experts, PAD, C), BF16)
    gathered = vmem((2, Y, X, R, C), BF16)
    ring = vmem((2, H, X, R, C), BF16)
    g1, g2 = pl.pallas_call(
        functools.partial(kernel, experts, Y),
        out_shape=(
            jax.ShapeDtypeStruct((width, hid), BF16),
            jax.ShapeDtypeStruct((hid, width), BF16),
        ),
        in_specs=[any_spec, any_spec, vmem_spec, vmem_spec, any_spec, any_spec, any_spec, any_spec],
        out_specs=(vmem_spec, vmem_spec),
        scratch_shapes=[
            vmem((2, tokens, C), BF16),
            vmem((width, hid), BF16),
            vmem((hid, width), BF16),
            vmem((width, hid), BF16),
            vmem((hid, width), BF16),
            vmem((2, tokens, experts * PAD), BF16),
            vmem((tokens, experts * PAD), BF16),
            message,
            message,
            message,
            message,
            message,
            message,
            gathered,
            gathered,
            gathered,
            gathered,
            gathered,
            vmem((Y, X, R, C), BF16),
            vmem((Y, X, R, C), BF16),
            ring,
            ring,
            ring,
            ring,
            vmem((2, X, R, C), F32),
            vmem((2, R, C), BF16),
            vmem((2, R, C), BF16),
            vmem((2 * R, hid), F32),
            vmem((2 * R, hid), BF16),
            dma((6,)),
            dma((3,)),
            dma((3,)),
            dma((3, 1 + 2 * H + Y)),
            dma((3, 2 + 2 * H)),
            dma((2, 2 + 2 * H)),
            dma((2, 2 + 2 * H)),
        ],
        compiler_params=pltpu.CompilerParams(
            collective_id=0, has_side_effects=True, vmem_limit_bytes=40 * 1024 * 1024
        ),
    )(teacher_in, student_in, teacher_route, student_route, w1t[0], w2t[0], w1s[0], w2s[0])
    return g1[None], g2[None]


def solution(mesh):
    return jax.shard_map(
        on_device,
        mesh=mesh,
        in_specs=(
            P("dp", None),
            P("dp", None),
            P("dp", None),
            P("dp", None),
            P("dp", None, "expert"),
            P("dp", "expert", None),
            P("dp", None, "expert"),
            P("dp", "expert", None),
        ),
        out_specs=(P("dp", None, "expert"), P("dp", "expert", None)),
        check_vma=False,
    )
```

```python
import functools
import math

import jax
import jax.numpy as jnp
from jax import lax
from jax.experimental import pallas as pl
from jax.experimental.pallas import tpu as pltpu
from jax.sharding import PartitionSpec as P

root_coef = math.sqrt(2.0 / math.pi)
cubic_coef = 0.044715
MESH = pl.DeviceIdType.MESH
F32 = jnp.float32
BF16 = jnp.bfloat16
CAP = 6
PAD = 16
X = 2


def gelu_tanh(pre_act):
    inner_arg = root_coef * (pre_act + cubic_coef * pre_act * pre_act * pre_act)
    return 0.5 * pre_act * (1.0 + jnp.tanh(inner_arg))


def gelu_slope(pre_act):
    tangent = jnp.tanh(root_coef * (pre_act + cubic_coef * pre_act * pre_act * pre_act))
    return 0.5 * (1.0 + tangent) + 0.5 * pre_act * (1.0 - tangent * tangent) * root_coef * (
        1.0 + 3.0 * cubic_coef * pre_act * pre_act
    )


def dot(a, b, ca=1, cb=0):
    return lax.dot_general(a, b, (((ca,), (cb,)), ((), ())), preferred_element_type=F32)


def iota(shape, dim):
    return lax.broadcasted_iota(jnp.int32, shape, dim)


def cat(parts, axis):
    return jnp.concatenate(parts, axis=axis)


def slot_rows(route):
    tokens = route.shape[1]
    member = (route == iota((128, tokens), 0)).astype(F32)
    earlier = (iota((tokens, tokens), 0) <= iota((tokens, tokens), 1)).astype(F32)
    rank = dot(member.astype(BF16), earlier.astype(BF16))
    position = jnp.sum(member * rank, axis=0, keepdims=True) - 1.0
    return route * PAD + position.astype(jnp.int32)


def kernel(
    experts,
    Y,
    xt_hbm,
    xs_hbm,
    rt_hbm,
    rs_hbm,
    w1t_hbm,
    w2t_hbm,
    w1s_hbm,
    w2s_hbm,
    g1_ref,
    g2_ref,
    xcol,
    routes,
    w1t,
    w2t,
    w1s,
    w2s,
    place,
    back,
    out1,
    in1,
    out2,
    in2,
    out3,
    in3,
    xt,
    xs,
    gr,
    part,
    ring,
    stage,
    finals,
    xsend,
    xland,
    ups,
    pre_ref,
    hid_ref,
    hid_own,
    hid_other,
    dpre_own,
    dpre_other,
    load_sem,
    w_send,
    w_recv,
    a_send,
    a_recv,
    g_send,
    g_recv,
    s_send,
    s_recv,
    r_send,
    r_recv,
):
    H = Y // 2
    tokens, C = xcol.shape[1], xcol.shape[2]
    R = experts * CAP
    Z = experts // 2
    many = experts // 2
    per = min(8, many)
    half = per * CAP
    G = R // 2
    me = lax.axis_index("dp")
    mine = lax.axis_index("expert")
    k, c = me // 2, me % 2
    z, far = k // 2, k % 2
    x, y = mine // Y, mine % Y

    here_x = x * Y
    sibling = (k * 2 + 1 - c, mine)
    across = (me, (1 - x) * Y + y)
    above = (me, here_x + (y + 1) % Y)
    below = (me, here_x + (y + Y - 1) % Y)

    def remote(src, dst, send, recv, device):
        return pltpu.make_async_remote_copy(
            src_ref=src, dst_ref=dst, send_sem=send, recv_sem=recv, device_id=device, device_id_type=MESH
        )

    started = []

    def go(copy):
        copy.start()
        started.append(copy)
        return copy

    barrier = pltpu.get_barrier_semaphore()

    def greet(j, carry):
        pl.semaphore_signal(
            barrier, inc=1, device_id=(((k + j) % experts) * 2 + c, mine), device_id_type=MESH
        )
        return carry

    lax.fori_loop(1, experts, greet, 0)
    for device in (sibling, across, above, below):
        pl.semaphore_signal(barrier, inc=1, device_id=device, device_id_type=MESH)

    def span(i):
        return pl.ds(pl.multiple_of(i * C, C), C), pl.ds(pl.multiple_of((Y + i) * C, C), C)

    weights = ((w1t_hbm, w1t), (w2t_hbm, w2t), (w1s_hbm, w1s), (w2s_hbm, w2s))
    loads = [
        pltpu.make_async_copy(rt_hbm, routes.at[0], load_sem.at[0]),
        pltpu.make_async_copy(rs_hbm, routes.at[1], load_sem.at[1]),
    ]
    for n, source in enumerate((xt_hbm, xs_hbm)):
        for i, columns in enumerate(span(y)):
            at = 2 * n + i
            loads.append(pltpu.make_async_copy(source.at[:, columns], xcol.at[at], load_sem.at[2 + at]))
    loads += [pltpu.make_async_copy(w, v.at[c], load_sem.at[6 + i]) for i, (w, v) in enumerate(weights)]
    for load in loads:
        load.start()

    rows = iota((experts * PAD, tokens), 0)

    def one_hot(slots):
        return (slots == rows).astype(F32)

    def to_blocks(n, a, b):
        lhs = cat([place[2 * n], place[2 * n + 1]], 1)
        return dot(lhs, cat([a, b], 0)).astype(BF16).reshape(experts, PAD, C)

    loads[0].wait()
    slot_t = slot_rows(routes[0])
    place[0] = one_hot(slot_t).astype(BF16)
    place[1] = one_hot(slot_t + CAP).astype(BF16)
    loads[2].wait()
    loads[3].wait()
    out1[0] = to_blocks(0, xcol[0], xcol[1])

    col = iota((2 * half, per * PAD), 1)
    block, lane = col // PAD, col % PAD
    target = jnp.where(
        lane < CAP,
        block * CAP + lane,
        jnp.where(lane < 2 * CAP, half + block * CAP + lane - CAP, -1),
    )
    pack = (iota((2 * half, per * PAD), 0) == target).astype(F32).astype(BF16)

    pl.semaphore_wait(barrier, experts - 1 + 4)

    def shift(r):
        i = r // 2
        odd = i % 2
        return odd * ((i + 1) // 2) + (1 - odd) * (Z - i // 2)

    def towards(r):
        return ((z + shift(r)) % Z) * 2 + (far + r) % 2

    def back_from(r):
        return ((z + 2 * Z - shift(r)) % Z) * 2 + (far + r) % 2

    def dispatch(n, src, dst):
        dst[0] = src[k]
        for g in range(2):

            def send(r, carry):
                other = towards(r)
                remote(
                    src.at[other], dst.at[r], a_send.at[n], a_recv.at[n, g], (other * 2 + c, mine)
                ).start()
                return carry

            lax.fori_loop(max(1, g * many), (g + 1) * many, send, 0)

    def wait_blocks(ref, count, sem):
        if count:
            blocks = ref.at[pl.ds(0, count)]
            pltpu.make_async_copy(blocks, blocks, sem).wait()

    def dispatch_wait(n, dst, g):
        wait_blocks(dst, many if g else many - 1, a_recv.at[n, g])

    def give_back(g):
        def send(r, carry):
            other = back_from(r)
            remote(
                out2.at[r], in2.at[k], a_send.at[3], a_recv.at[3, 0], (other * 2 + c, mine)
            ).start()
            return carry

        lax.fori_loop(max(1, g * many), (g + 1) * many, send, 0)
        if g == 0:
            in2[k] = out2[0]

    def group_rows(g):
        return pl.ds(g * G, G)

    def split_rows(g, way):
        return pl.ds(g * G + way * (G // 2), G // 2)

    class Gather:
        def __init__(self, n, buf, g):
            self.n, self.buf, self.g = n, buf, g
            self.ring = {}

        def send(self, way, s):
            from_y = (y + Y - (s - 1)) % Y if way == 0 else (y + s - 1) % Y
            rows = group_rows(self.g) if s < H else split_rows(self.g, way)
            chunk = self.buf.at[from_y, :, rows]
            i = way * H + s - 1
            self.ring[way, s] = go(
                remote(chunk, chunk, g_send.at[self.n, i], g_recv.at[self.n, i], above if way == 0 else below)
            )

        def step(self, s):
            if s == 0:
                self.send(0, 1)
                self.send(1, 1)
                return
            for way in (0, 1):
                self.ring[way, s].wait_recv()
                if s < H:
                    self.send(way, s + 1)

    def arrived(s):
        if s == 0:
            return [y]
        if s == H:
            return [(y + H) % Y]
        return [(y + Y - s) % Y, (y + s) % Y]

    def pack_rows(src, g):
        for b in range(many // per):
            blocks = src[pl.ds(g * many + b * per, per)].reshape(per * PAD, C)
            packed = dot(pack, blocks)
            yield pl.ds(g * G + b * half, half), packed[:half], packed[half:]

    def unpack_in(src, g, dst):
        for rows, first, second in pack_rows(src, g):
            dst[y, 0, rows] = first.astype(BF16)
            dst[y, 1, rows] = second.astype(BF16)

    def w1_rows(w, i):
        a, b = span(i)
        return cat([cat([w[0, a], w[1, a]], 1), cat([w[0, b], w[1, b]], 1)], 0)

    def w2_cols(w, i):
        a, b = span(i)
        return cat([cat([w[0, :, a], w[0, :, b]], 1), cat([w[1, :, a], w[1, :, b]], 1)], 0)

    def pair(buf, i):
        return cat([buf[i, 0], buf[i, 1]], 1)

    def add_pre(n, s):
        buf, w = ((xt, w1t), (xs.at[c], w1s))[n]
        total = pre_ref[n] if s else None
        for i in arrived(s):
            product = dot(pair(buf, i), w1_rows(w, i))
            total = product if total is None else total + product
        pre_ref[n] = total

    dispatch(0, out1.at[0], in1.at[0])
    swaps = [go(remote(w, v.at[c], w_send.at[i], w_recv.at[i], sibling)) for i, (w, v) in enumerate(weights)]
    loads[1].wait()
    slot_s = slot_rows(routes[1])
    place[2] = one_hot(slot_s).astype(BF16)
    place[3] = one_hot(slot_s + CAP).astype(BF16)
    loads[4].wait()
    loads[5].wait()
    out1[1] = to_blocks(1, xcol[2], xcol[3])
    dispatch(1, out1.at[1], in1.at[1])
    back[0] = jnp.transpose(one_hot(slot_t)).astype(BF16)
    back[1] = jnp.transpose(one_hot(slot_t + CAP)).astype(BF16)

    gather_t = [Gather(g, xt, g) for g in range(2)]
    for g in range(2):
        dispatch_wait(0, in1.at[0], g)
        unpack_in(in1.at[0], g, xt)
        gather_t[g].step(0)
    loads[6].wait()
    swaps[0].wait_recv()
    add_pre(0, 0)
    for s in range(1, H):
        gather_t[0].step(s)
        gather_t[1].step(s)
        add_pre(0, s)
    gather_t[0].step(H)
    gather_t[1].step(H)

    def slot(d):
        return 0 if d == H else 2 * (H - abs(d)) - (1 if d > 0 else 0) if d else 2 * H - 1

    def make_part(n, d):
        i = (y + Y + d) % Y
        out = dot(hid_ref[n], w2_cols((w2t, w2s)[n], i))
        part[n, slot(d), 0] = out[:, :C]
        part[n, slot(d), 1] = out[:, C:]

    class Scatter:
        def __init__(self, n, g):
            self.n, self.g, self.m = n, g, 2 * n + g
            self.copies = {}

        def send(self, way, s):
            rows = group_rows(self.g) if s > 1 else split_rows(self.g, way)
            src, dst = stage.at[self.n, way, s - 1, :, rows], ring.at[self.n, way, s - 1, :, rows]
            i = way * H + s - 1
            self.copies[way, s] = go(
                remote(src, dst, r_send.at[self.m, i], r_recv.at[self.m, i], above if way == 0 else below)
            )

        def step(self, s):
            n = self.n
            if s == 1:
                rows = group_rows(self.g)
                stage[n, 0, 0, :, rows] = part[n, 0, :, rows].astype(BF16)
                stage[n, 1, 0, :, rows] = part[n, 0, :, rows].astype(BF16)
                self.send(0, 1)
                self.send(1, 1)
                return
            d = H + 1 - s
            for way in (0, 1):
                at = slot(d if way == 0 else -d)
                self.copies[way, s - 1].wait_recv()
                for w in (0, 1):
                    rows = split_rows(self.g, w)
                    total = part[n, at, :, rows]
                    if s > 2 or w == way:
                        total = total + ring[n, way, s - 2, :, rows].astype(F32)
                    stage[n, way, s - 1, :, rows] = total.astype(BF16)
                self.send(way, s)

        def last(self):
            n, rows = self.n, group_rows(self.g)
            total = part[n, slot(0), :, rows]
            for way in (0, 1):
                self.copies[way, H].wait_recv()
                total = total + ring[n, way, H - 1, :, rows].astype(F32)
            return total

    def far_parts(n, s):
        for d in (H + 1 - s, s - H - 1):
            make_part(n, d)

    def scatter_step(n, s):
        for g in (1, 0):
            scatters[n][g].step(s)

    scatters = [[Scatter(n, g) for g in range(2)] for n in (0, 1)]
    gather_s = [Gather(2 + g, xs.at[c], g) for g in range(2)]

    add_pre(0, H)
    hid_ref[0] = gelu_tanh(pre_ref[0]).astype(BF16)
    loads[7].wait()
    swaps[1].wait_recv()
    make_part(0, H)
    scatter_step(0, 1)
    for g in range(2):
        dispatch_wait(1, in1.at[1], g)
        unpack_in(in1.at[1], g, xs.at[c])
        gather_s[g].step(0)
    loads[8].wait()
    swaps[2].wait_recv()
    for s in range(2, H + 1):
        far_parts(0, s)
        scatter_step(0, s)
        gather_s[0].step(s - 1)
        gather_s[1].step(s - 1)
        add_pre(1, s - 2)
    make_part(0, 0)
    for g in (1, 0):
        total = scatters[0][g].last().astype(BF16)
        for b in range(many // per):
            rows_b = slice(b * half, (b + 1) * half)
            spread = dot(pack, cat([total[0, rows_b], total[1, rows_b]], 0), 0, 0)
            out2[pl.ds(g * many + b * per, per)] = spread.astype(BF16).reshape(per, PAD, C)
        give_back(g)

    gather_s[0].step(H)
    gather_s[1].step(H)
    add_pre(1, H - 1)
    add_pre(1, H)
    hid_ref[1] = gelu_tanh(pre_ref[1]).astype(BF16)
    loads[9].wait()
    swaps[3].wait_recv()
    make_part(1, H)
    scatter_step(1, 1)
    hid_own[0] = hid_ref[1, :, :C]
    hid_own[1] = hid_ref[1, :, C:]
    hid_swap = go(remote(hid_own.at[1 - c], hid_other, s_send.at[0], s_recv.at[0], sibling))
    xs_swap = go(remote(xs.at[c], xs.at[c], s_send.at[1], s_recv.at[1], sibling))
    far_parts(1, 2)
    scatter_step(1, 2)
    for s in range(3, H + 1):
        far_parts(1, s)
    make_part(1, 0)

    wait_blocks(in2, experts - 1, a_recv.at[3, 0])
    came = in2[...].reshape(experts * PAD, C)
    mine_t = [dot(back[i], came) for i in (0, 1)]
    for i in (0, 1):
        ups[0, i] = mine_t[i].astype(BF16)
    up_swap = go(remote(ups.at[0], ups.at[1], s_send.at[2], s_recv.at[2], across))
    for s in range(3, H):
        scatter_step(1, s)
    up_swap.wait_recv()
    full_t = [(mine_t[i] + ups[1, i].astype(F32)).astype(BF16) for i in (0, 1)]
    out3[...] = to_blocks(1, full_t[0], full_t[1])
    dispatch(2, out3, in3)
    if H > 2:
        scatter_step(1, H)
    x_swaps = []
    for g in (1, 0):
        total = scatters[1][g].last()
        finals[:, group_rows(g)] = total
        xsend[:, group_rows(g)] = total.astype(BF16)
        x_swaps.append(
            go(
                remote(
                    xsend.at[:, group_rows(g)],
                    xland.at[:, group_rows(g)],
                    s_send.at[5 + g],
                    s_recv.at[5 + g],
                    across,
                )
            )
        )
    for copy in x_swaps:
        copy.wait_recv()

    sib_sent = [0]

    def to_sibling(i, rows):
        chunk = gr.at[c, i, :, rows]
        at = 7 + sib_sent[0]
        sib_sent[0] += 1
        go(remote(chunk, chunk, s_send.at[at], s_recv.at[3], sibling))

    gather_g = [Gather(4 + g, gr.at[c], g) for g in range(2)]

    def grad_step(g, s):
        gather_g[g].step(s)
        for i in arrived(s):
            to_sibling(i, group_rows(g))

    def add_hidden_grad(i, total):
        product = dot(pair(gr.at[c], i), w2_cols(w2s, i), 1, 1)
        return product if total is None else total + product

    scale = 1.0 / math.sqrt(tokens)
    for g in range(2):
        dispatch_wait(2, in3, g)
        for rows_b, first, second in pack_rows(in3, g):
            for i, value in ((0, first), (1, second)):
                student = finals[i, rows_b] + xland[i, rows_b].astype(F32)
                gr[c, y, i, rows_b] = ((student - value) * scale).astype(BF16)
        grad_step(g, 0)
    hidden_grad = add_hidden_grad(y, None)
    for s in range(1, H + 1):
        grad_step(0, s)
        grad_step(1, s)
        for i in arrived(s):
            hidden_grad = add_hidden_grad(i, hidden_grad)
    pre_grad = (hidden_grad * gelu_slope(pre_ref[1])).astype(BF16)
    dpre_own[0] = pre_grad[:, :C]
    dpre_own[1] = pre_grad[:, C:]
    dpre_swap = go(remote(dpre_own.at[1 - c], dpre_other, s_send.at[3], s_recv.at[4], sibling))

    hid_swap.wait_recv()
    whole = gr.at[1 - c]
    pltpu.make_async_copy(whole, whole, s_recv.at[3]).wait()
    hidden_all = cat([hid_own[c], hid_other[...]], 0)

    def back_second(i, carry):
        a, b = span(i)
        out = dot(hidden_all, cat([pair(gr.at[c], i), pair(gr.at[1 - c], i)], 0), 0, 0).astype(BF16)
        g2_ref[:, a] = out[:, :C]
        g2_ref[:, b] = out[:, C:]
        return carry

    lax.fori_loop(0, Y, back_second, 0)
    xs_swap.wait_recv()
    dpre_swap.wait_recv()
    pre_grad_all = cat([dpre_own[c], dpre_other[...]], 0)

    def back_first(i, carry):
        a, b = span(i)
        out = dot(cat([pair(xs.at[c], i), pair(xs.at[1 - c], i)], 0), pre_grad_all, 0, 0).astype(BF16)
        g1_ref[a] = out[:C]
        g1_ref[b] = out[C:]
        return carry

    lax.fori_loop(0, Y, back_first, 0)

    for copy in started:
        copy.wait_send()
    for n, src in ((0, out1.at[0]), (1, out1.at[1]), (2, out3), (3, out2)):
        wait_blocks(src, experts - 1, a_send.at[n])


def on_device(teacher_in, student_in, teacher_route, student_route, w1t, w2t, w1s, w2s):
    experts = lax.axis_size("dp") // 2
    spots = lax.axis_size("expert")
    Y = spots // X
    H = Y // 2
    tokens, width = teacher_in.shape
    C = width // spots
    hid = w1t.shape[2]
    R = experts * CAP
    vmem, dma = pltpu.VMEM, pltpu.SemaphoreType.DMA
    hbm_spec, vmem_spec = pl.BlockSpec(memory_space=pltpu.HBM), pl.BlockSpec(memory_space=vmem)
    message = vmem((experts, PAD, C), BF16)
    around = vmem((2, 2, H, X, R, C), BF16)
    g1, g2 = pl.pallas_call(
        functools.partial(kernel, experts, Y),
        out_shape=(
            jax.ShapeDtypeStruct((width, hid), BF16),
            jax.ShapeDtypeStruct((hid, width), BF16),
        ),
        in_specs=[hbm_spec] * 8,
        out_specs=(vmem_spec, vmem_spec),
        scratch_shapes=[
            vmem((4, tokens, C), BF16),
            vmem((2, 1, tokens), jnp.int32),
            vmem((2, width, hid), BF16),
            vmem((2, hid, width), BF16),
            vmem((2, width, hid), BF16),
            vmem((2, hid, width), BF16),
            vmem((4, experts * PAD, tokens), BF16),
            vmem((2, tokens, experts * PAD), BF16),
            vmem((2, experts, PAD, C), BF16),
            vmem((2, experts, PAD, C), BF16),
            message,
            message,
            message,
            message,
            vmem((Y, X, R, C), BF16),
            vmem((2, Y, X, R, C), BF16),
            vmem((2, Y, X, R, C), BF16),
            vmem((2, Y, X, R, C), F32),
            around,
            around,
            vmem((X, R, C), F32),
            vmem((X, R, C), BF16),
            vmem((X, R, C), BF16),
            vmem((2, X, tokens, C), BF16),
            vmem((2, R, 2 * hid), F32),
            vmem((2, R, 2 * hid), BF16),
            vmem((2, R, hid), BF16),
            vmem((R, hid), BF16),
            vmem((2, R, hid), BF16),
            vmem((R, hid), BF16),
            dma((10,)),
            dma((4,)),
            dma((4,)),
            dma((4,)),
            dma((4, 2)),
            dma((6, 2 * H)),
            dma((6, 2 * H)),
            dma((7 + 2 * Y,)),
            dma((7,)),
            dma((4, 2 * H)),
            dma((4, 2 * H)),
        ],
        compiler_params=pltpu.CompilerParams(
            collective_id=0, has_side_effects=True, vmem_limit_bytes=63 * 1024 * 1024
        ),
    )(
        teacher_in,
        student_in,
        teacher_route.reshape(1, tokens),
        student_route.reshape(1, tokens),
        w1t[0],
        w2t[0],
        w1s[0],
        w2s[0],
    )
    return g1[None], g2[None]


def solution(mesh):
    return jax.shard_map(
        on_device,
        mesh=mesh,
        in_specs=(
            P("dp", None),
            P("dp", None),
            P("dp", None),
            P("dp", None),
            P("dp", None, "expert"),
            P("dp", "expert", None),
            P("dp", None, "expert"),
            P("dp", "expert", None),
        ),
        out_specs=(P("dp", None, "expert"), P("dp", "expert", None)),
        check_vma=False,
    )
```

```python
import functools
import math

import jax
import jax.numpy as jnp
from jax import lax
from jax.experimental import pallas as pl
from jax.experimental.pallas import tpu as pltpu
from jax.sharding import PartitionSpec as P

root_coef = math.sqrt(2.0 / math.pi)
cubic_coef = 0.044715
MESH = pl.DeviceIdType.MESH
F32 = jnp.float32
BF16 = jnp.bfloat16
CAP = 6
PAD = 16
X = 2


def gelu_tanh(pre_act):
    inner_arg = root_coef * (pre_act + cubic_coef * pre_act * pre_act * pre_act)
    return 0.5 * pre_act * (1.0 + jnp.tanh(inner_arg))


def gelu_slope(pre_act):
    tangent = jnp.tanh(root_coef * (pre_act + cubic_coef * pre_act * pre_act * pre_act))
    return 0.5 * (1.0 + tangent) + 0.5 * pre_act * (1.0 - tangent * tangent) * root_coef * (
        1.0 + 3.0 * cubic_coef * pre_act * pre_act
    )


def dot(a, b, ca=1, cb=0):
    return lax.dot_general(a, b, (((ca,), (cb,)), ((), ())), preferred_element_type=F32)


def iota(shape, dim):
    return lax.broadcasted_iota(jnp.int32, shape, dim)


def cat(parts, axis):
    return jnp.concatenate(parts, axis=axis)


def slot_rows(route):
    tokens = route.shape[1]
    member = (route == iota((128, tokens), 0)).astype(F32)
    earlier = (iota((tokens, tokens), 0) <= iota((tokens, tokens), 1)).astype(F32)
    rank = dot(member.astype(BF16), earlier.astype(BF16))
    position = jnp.sum(member * rank, axis=0, keepdims=True) - 1.0
    return route * PAD + position.astype(jnp.int32)


def kernel(
    experts,
    Y,
    xt_hbm,
    xs_hbm,
    rt_hbm,
    rs_hbm,
    w1t_hbm,
    w2t_hbm,
    w1s_hbm,
    w2s_hbm,
    g1_ref,
    g2_ref,
    xcol,
    routes,
    w1t,
    w2t,
    w1s,
    w2s,
    place,
    back,
    out1,
    in1,
    out2,
    in2,
    out3,
    in3,
    xt,
    xs,
    gr,
    part,
    ring,
    stage,
    finals,
    xsend,
    xland,
    ups,
    pre_ref,
    hid_ref,
    hid_own,
    hid_other,
    dpre_own,
    dpre_other,
    hid_turned,
    xs_turned,
    load_sem,
    w_send,
    w_recv,
    a_send,
    a_recv,
    g_send,
    g_recv,
    s_send,
    s_recv,
    r_send,
    r_recv,
):
    H = Y // 2
    tokens, C = xcol.shape[1], xcol.shape[2]
    R = experts * CAP
    Z = experts // 2
    many = experts // 2
    per = min(8, many)
    half = per * CAP
    G = R // 2
    me = lax.axis_index("dp")
    mine = lax.axis_index("expert")
    k, c = me // 2, me % 2
    z, far = k // 2, k % 2
    x, y = mine // Y, mine % Y

    here_x = x * Y
    sibling = (k * 2 + 1 - c, mine)
    across = (me, (1 - x) * Y + y)
    above = (me, here_x + (y + 1) % Y)
    below = (me, here_x + (y + Y - 1) % Y)
    above2 = (me, here_x + (y + 2) % Y)
    below2 = (me, here_x + (y + Y - 2) % Y)

    def remote(src, dst, send, recv, device):
        return pltpu.make_async_remote_copy(
            src_ref=src, dst_ref=dst, send_sem=send, recv_sem=recv, device_id=device, device_id_type=MESH
        )

    started = []

    def go(copy):
        copy.start()
        started.append(copy)
        return copy

    barrier = pltpu.get_barrier_semaphore()

    def greet(j, carry):
        pl.semaphore_signal(
            barrier, inc=1, device_id=(((k + j) % experts) * 2 + c, mine), device_id_type=MESH
        )
        return carry

    lax.fori_loop(1, experts, greet, 0)
    for device in (sibling, across, above, below, above2, below2):
        pl.semaphore_signal(barrier, inc=1, device_id=device, device_id_type=MESH)

    def span(i):
        return pl.ds(pl.multiple_of(i * C, C), C), pl.ds(pl.multiple_of((Y + i) * C, C), C)

    weights = ((w1t_hbm, w1t), (w2t_hbm, w2t), (w1s_hbm, w1s), (w2s_hbm, w2s))
    loads = [
        pltpu.make_async_copy(rt_hbm, routes.at[0], load_sem.at[0]),
        pltpu.make_async_copy(rs_hbm, routes.at[1], load_sem.at[1]),
    ]
    for n, source in enumerate((xt_hbm, xs_hbm)):
        for i, columns in enumerate(span(y)):
            at = 2 * n + i
            loads.append(pltpu.make_async_copy(source.at[:, columns], xcol.at[at], load_sem.at[2 + at]))
    loads += [pltpu.make_async_copy(w, v.at[c], load_sem.at[6 + i]) for i, (w, v) in enumerate(weights)]
    for load in loads:
        load.start()

    rows = iota((experts * PAD, tokens), 0)

    def one_hot(slots):
        return (slots == rows).astype(F32)

    def to_blocks(n, a, b):
        lhs = cat([place[2 * n], place[2 * n + 1]], 1)
        return dot(lhs, cat([a, b], 0)).astype(BF16).reshape(experts, PAD, C)

    loads[0].wait()
    slot_t = slot_rows(routes[0])
    place[0] = one_hot(slot_t).astype(BF16)
    place[1] = one_hot(slot_t + CAP).astype(BF16)
    loads[2].wait()
    loads[3].wait()
    out1[0] = to_blocks(0, xcol[0], xcol[1])

    col = iota((2 * half, per * PAD), 1)
    block, lane = col // PAD, col % PAD
    target = jnp.where(
        lane < CAP,
        block * CAP + lane,
        jnp.where(lane < 2 * CAP, half + block * CAP + lane - CAP, -1),
    )
    pack = (iota((2 * half, per * PAD), 0) == target).astype(F32).astype(BF16)

    pl.semaphore_wait(barrier, experts - 1 + 6)

    def shift(r):
        i = r // 2
        odd = i % 2
        return odd * ((i + 1) // 2) + (1 - odd) * (Z - i // 2)

    def towards(r):
        return ((z + shift(r)) % Z) * 2 + (far + r) % 2

    def back_from(r):
        return ((z + 2 * Z - shift(r)) % Z) * 2 + (far + r) % 2

    def dispatch(n, src, dst):
        dst[0] = src[k]
        for g in (1, 0):

            def send(j, carry):
                r = (g + 1) * many - 1 - j
                other = towards(r)
                remote(
                    src.at[other], dst.at[r], a_send.at[n], a_recv.at[n, g], (other * 2 + c, mine)
                ).start()
                return carry

            lax.fori_loop(0, many if g else many - 1, send, 0)

    def wait_blocks(ref, count, sem):
        if count:
            blocks = ref.at[pl.ds(0, count)]
            pltpu.make_async_copy(blocks, blocks, sem).wait()

    def dispatch_wait(n, dst, g):
        wait_blocks(dst, many if g else many - 1, a_recv.at[n, g])

    def give_back(g):
        def send(j, carry):
            r = (g + 1) * many - 1 - j
            other = back_from(r)
            remote(
                out2.at[r], in2.at[k], a_send.at[3], a_recv.at[3, 0], (other * 2 + c, mine)
            ).start()
            return carry

        lax.fori_loop(0, many if g else many - 1, send, 0)
        if g == 0:
            in2[k] = out2[0]

    def group_rows(g):
        return pl.ds(g * G, G)

    def split_rows(g, way):
        return pl.ds(g * G + way * (G // 2), G // 2)

    class Gather:
        def __init__(self, n, buf, g):
            self.n, self.buf, self.g = n, buf, g
            self.ring = {}

        def send(self, way, s, to, rows, device):
            from_y = (y + Y - s) % Y if way == 0 else (y + s) % Y
            chunk = self.buf.at[from_y, :, rows]
            i = way * H + to - 1
            self.ring[way, to] = go(remote(chunk, chunk, g_send.at[self.n, i], g_recv.at[self.n, i], device))

        def step(self, s):
            for way in (0, 1):
                if s:
                    self.ring[way, s].wait_recv()
                if s < H - 1:
                    self.send(way, s, s + 1, group_rows(self.g), (above, below)[way])
                if s == H - 2:
                    self.send(way, s, H, split_rows(self.g, way), (above2, below2)[way])

    def arrived(s):
        if s == 0:
            return [y]
        if s == H:
            return [(y + H) % Y]
        return [(y + Y - s) % Y, (y + s) % Y]

    def pack_rows(src, g):
        for b in range(many // per):
            blocks = src[pl.ds(g * many + b * per, per)].reshape(per * PAD, C)
            packed = dot(pack, blocks)
            yield pl.ds(g * G + b * half, half), packed[:half], packed[half:]

    def unpack_in(src, g, dst):
        for rows, first, second in pack_rows(src, g):
            dst[y, 0, rows] = first.astype(BF16)
            dst[y, 1, rows] = second.astype(BF16)

    def w1_rows(w, i):
        a, b = span(i)
        return cat([cat([w[0, a], w[1, a]], 1), cat([w[0, b], w[1, b]], 1)], 0)

    def w2_cols(w, i):
        a, b = span(i)
        return cat([cat([w[0, :, a], w[0, :, b]], 1), cat([w[1, :, a], w[1, :, b]], 1)], 0)

    def pair(buf, i):
        return cat([buf[i, 0], buf[i, 1]], 1)

    def add_pre(n, s):
        buf, w = ((xt, w1t), (xs.at[c], w1s))[n]
        total = pre_ref[n] if s else None
        for i in arrived(s):
            product = dot(pair(buf, i), w1_rows(w, i))
            total = product if total is None else total + product
        pre_ref[n] = total

    dispatch(0, out1.at[0], in1.at[0])
    swaps = [go(remote(w, v.at[c], w_send.at[i], w_recv.at[i], sibling)) for i, (w, v) in enumerate(weights)]
    loads[1].wait()
    slot_s = slot_rows(routes[1])
    place[2] = one_hot(slot_s).astype(BF16)
    place[3] = one_hot(slot_s + CAP).astype(BF16)
    loads[4].wait()
    loads[5].wait()
    out1[1] = to_blocks(1, xcol[2], xcol[3])
    dispatch(1, out1.at[1], in1.at[1])
    back[0] = jnp.transpose(one_hot(slot_t)).astype(BF16)
    back[1] = jnp.transpose(one_hot(slot_t + CAP)).astype(BF16)

    gather_t = [Gather(g, xt, g) for g in range(2)]
    for g in range(2):
        dispatch_wait(0, in1.at[0], g)
        unpack_in(in1.at[0], g, xt)
        gather_t[g].step(0)
    loads[6].wait()
    swaps[0].wait_recv()
    add_pre(0, 0)
    for s in range(1, H):
        gather_t[0].step(s)
        gather_t[1].step(s)
        add_pre(0, s)
    gather_t[0].step(H)
    gather_t[1].step(H)
    add_pre(0, H)

    def slot(d):
        return 0 if d == H else 2 * (H - abs(d)) - (1 if d > 0 else 0) if d else 2 * H - 1

    def make_part(n, d):
        i = (y + Y + d) % Y
        out = dot(hid_ref[n], w2_cols((w2t, w2s)[n], i))
        part[n, slot(d), 0] = out[:, :C]
        part[n, slot(d), 1] = out[:, C:]

    class Scatter:
        def __init__(self, n, g):
            self.n, self.g, self.m = n, g, 2 * n + g
            self.copies = {}

        def send(self, way, i, rows, device):
            src, dst = stage.at[self.n, way, i, :, rows], ring.at[self.n, way, i, :, rows]
            at = way * H + i
            self.copies[way, i] = go(remote(src, dst, r_send.at[self.m, at], r_recv.at[self.m, at], device))

        def halves(self):
            for way in (0, 1):
                rows = split_rows(self.g, way)
                stage[self.n, way, H - 1, :, rows] = part[self.n, slot(H), :, rows].astype(BF16)
                self.send(way, H - 1, rows, (above2, below2)[way])

        def step(self, s, way):
            n, d = self.n, H - s
            at = slot(d if way == 0 else -d)
            if s > 1:
                self.copies[way, s - 2].wait_recv()
            if s == 2:
                self.copies[way, H - 1].wait_recv()
            for w in (0, 1):
                rows = split_rows(self.g, w)
                total = part[n, at, :, rows]
                if s > 1:
                    total = total + ring[n, way, s - 2, :, rows].astype(F32)
                if s == 2 and w == way:
                    total = total + ring[n, way, H - 1, :, rows].astype(F32)
                stage[n, way, s - 1, :, rows] = total.astype(BF16)
            self.send(way, s - 1, group_rows(self.g), (above, below)[way])

        def last(self):
            n, rows = self.n, group_rows(self.g)
            total = part[n, slot(0), :, rows]
            for way in (0, 1):
                self.copies[way, H - 2].wait_recv()
                total = total + ring[n, way, H - 2, :, rows].astype(F32)
            return total

    def far_parts(n, s):
        for d in (H - s, s - H):
            make_part(n, d)

    def scatter_step(n, s):
        for g in (1, 0):
            for way in (0, 1):
                scatters[n][g].step(s, way)

    def scatter_start(n):
        for way in (0, 1):
            make_part(n, (1 - 2 * way) * (H - 1))
            for g in (1, 0):
                scatters[n][g].step(1, way)
        make_part(n, H)
        for g in (1, 0):
            scatters[n][g].halves()

    scatters = [[Scatter(n, g) for g in range(2)] for n in (0, 1)]
    gather_s = [Gather(2 + g, xs.at[c], g) for g in range(2)]

    hid_ref[0] = gelu_tanh(pre_ref[0]).astype(BF16)
    loads[7].wait()
    swaps[1].wait_recv()
    scatter_start(0)
    for g in range(2):
        dispatch_wait(1, in1.at[1], g)
        unpack_in(in1.at[1], g, xs.at[c])
        gather_s[g].step(0)
    loads[8].wait()
    swaps[2].wait_recv()
    for s in range(2, H):
        far_parts(0, s)
        scatter_step(0, s)
        gather_s[0].step(s - 1)
        gather_s[1].step(s - 1)
        add_pre(1, s - 2)
    make_part(0, 0)
    for g in (1, 0):
        total = scatters[0][g].last().astype(BF16)
        for b in range(many // per):
            rows_b = slice(b * half, (b + 1) * half)
            spread = dot(pack, cat([total[0, rows_b], total[1, rows_b]], 0), 0, 0)
            out2[pl.ds(g * many + b * per, per)] = spread.astype(BF16).reshape(per, PAD, C)
        give_back(g)

    for s in (H - 1, H):
        gather_s[0].step(s)
        gather_s[1].step(s)
    add_pre(1, H - 2)
    add_pre(1, H - 1)
    add_pre(1, H)
    hid_ref[1] = gelu_tanh(pre_ref[1]).astype(BF16)
    loads[9].wait()
    swaps[3].wait_recv()
    scatter_start(1)
    hid_own[0] = hid_ref[1, :, :C]
    hid_own[1] = hid_ref[1, :, C:]
    hid_swap = go(remote(hid_own.at[1 - c], hid_other, s_send.at[0], s_recv.at[0], sibling))
    xs_swap = go(remote(xs.at[c], xs.at[c], s_send.at[1], s_recv.at[1], sibling))
    for s in range(2, H):
        far_parts(1, s)
    make_part(1, 0)

    wait_blocks(in2, experts - 1, a_recv.at[3, 0])
    came = in2[...].reshape(experts * PAD, C)
    mine_t = [dot(back[i], came) for i in (0, 1)]
    for i in (0, 1):
        ups[0, i] = mine_t[i].astype(BF16)
    up_swap = go(remote(ups.at[0], ups.at[1], s_send.at[2], s_recv.at[2], across))
    scatter_step(1, 2)
    up_swap.wait_recv()
    full_t = [(mine_t[i] + ups[1, i].astype(F32)).astype(BF16) for i in (0, 1)]
    out3[...] = to_blocks(1, full_t[0], full_t[1])
    dispatch(2, out3, in3)
    for s in range(3, H):
        scatter_step(1, s)
    x_swaps = []
    for g in (1, 0):
        total = scatters[1][g].last()
        finals[:, group_rows(g)] = total
        xsend[:, group_rows(g)] = total.astype(BF16)
        x_swaps.append(
            go(
                remote(
                    xsend.at[:, group_rows(g)],
                    xland.at[:, group_rows(g)],
                    s_send.at[5 + g],
                    s_recv.at[5 + g],
                    across,
                )
            )
        )

    hid_swap.wait_recv()
    hid_turned[...] = jnp.transpose(cat([hid_own[c], hid_other[...]], 0).astype(F32)).astype(BF16)
    xs_swap.wait_recv()

    def turn(i, carry):
        rows_i = cat([pair(xs.at[c], i), pair(xs.at[1 - c], i)], 0)
        xs_turned[i] = jnp.transpose(rows_i.astype(F32)).astype(BF16)
        return carry

    lax.fori_loop(0, Y, turn, 0)
    for copy in x_swaps:
        copy.wait_recv()

    sib_sent = [0]

    def to_sibling(i, rows):
        chunk = gr.at[c, i, :, rows]
        at = 7 + sib_sent[0]
        sib_sent[0] += 1
        go(remote(chunk, chunk, s_send.at[at], s_recv.at[3], sibling))

    gather_g = [Gather(4 + g, gr.at[c], g) for g in range(2)]

    def grad_step(g, s):
        gather_g[g].step(s)
        for i in arrived(s):
            to_sibling(i, group_rows(g))

    def add_hidden_grad(i, total):
        product = dot(pair(gr.at[c], i), w2_cols(w2s, i), 1, 1)
        return product if total is None else total + product

    scale = 1.0 / math.sqrt(tokens)
    for g in range(2):
        dispatch_wait(2, in3, g)
        for rows_b, first, second in pack_rows(in3, g):
            for i, value in ((0, first), (1, second)):
                student = finals[i, rows_b] + xland[i, rows_b].astype(F32)
                gr[c, y, i, rows_b] = ((student - value) * scale).astype(BF16)
        grad_step(g, 0)
    hidden_grad = add_hidden_grad(y, None)
    for s in range(1, H + 1):
        grad_step(0, s)
        grad_step(1, s)
        for i in arrived(s):
            hidden_grad = add_hidden_grad(i, hidden_grad)
    pre_grad = (hidden_grad * gelu_slope(pre_ref[1])).astype(BF16)
    dpre_own[0] = pre_grad[:, :C]
    dpre_own[1] = pre_grad[:, C:]
    dpre_swap = go(remote(dpre_own.at[1 - c], dpre_other, s_send.at[3], s_recv.at[4], sibling))

    whole = gr.at[1 - c]
    pltpu.make_async_copy(whole, whole, s_recv.at[3]).wait()

    def back_second(i, carry):
        a, b = span(i)
        out = dot(hid_turned[...], cat([pair(gr.at[c], i), pair(gr.at[1 - c], i)], 0)).astype(BF16)
        g2_ref[:, a] = out[:, :C]
        g2_ref[:, b] = out[:, C:]
        return carry

    lax.fori_loop(0, Y, back_second, 0)
    dpre_swap.wait_recv()
    pre_grad_all = cat([dpre_own[c], dpre_other[...]], 0)

    def back_first(i, carry):
        a, b = span(i)
        out = dot(xs_turned[i], pre_grad_all).astype(BF16)
        g1_ref[a] = out[:C]
        g1_ref[b] = out[C:]
        return carry

    lax.fori_loop(0, Y, back_first, 0)

    for copy in started:
        copy.wait_send()
    for n, src in ((0, out1.at[0]), (1, out1.at[1]), (2, out3), (3, out2)):
        wait_blocks(src, experts - 1, a_send.at[n])


def on_device(teacher_in, student_in, teacher_route, student_route, w1t, w2t, w1s, w2s):
    experts = lax.axis_size("dp") // 2
    spots = lax.axis_size("expert")
    Y = spots // X
    H = Y // 2
    tokens, width = teacher_in.shape
    C = width // spots
    hid = w1t.shape[2]
    R = experts * CAP
    vmem, dma = pltpu.VMEM, pltpu.SemaphoreType.DMA
    hbm_spec, vmem_spec = pl.BlockSpec(memory_space=pltpu.HBM), pl.BlockSpec(memory_space=vmem)
    message = vmem((experts, PAD, C), BF16)
    around = vmem((2, 2, H, X, R, C), BF16)
    g1, g2 = pl.pallas_call(
        functools.partial(kernel, experts, Y),
        out_shape=(
            jax.ShapeDtypeStruct((width, hid), BF16),
            jax.ShapeDtypeStruct((hid, width), BF16),
        ),
        in_specs=[hbm_spec] * 8,
        out_specs=(vmem_spec, vmem_spec),
        scratch_shapes=[
            vmem((4, tokens, C), BF16),
            vmem((2, 1, tokens), jnp.int32),
            vmem((2, width, hid), BF16),
            vmem((2, hid, width), BF16),
            vmem((2, width, hid), BF16),
            vmem((2, hid, width), BF16),
            vmem((4, experts * PAD, tokens), BF16),
            vmem((2, tokens, experts * PAD), BF16),
            vmem((2, experts, PAD, C), BF16),
            vmem((2, experts, PAD, C), BF16),
            message,
            message,
            message,
            message,
            vmem((Y, X, R, C), BF16),
            vmem((2, Y, X, R, C), BF16),
            vmem((2, Y, X, R, C), BF16),
            vmem((2, Y, X, R, C), F32),
            around,
            around,
            vmem((X, R, C), F32),
            vmem((X, R, C), BF16),
            vmem((X, R, C), BF16),
            vmem((2, X, tokens, C), BF16),
            vmem((2, R, 2 * hid), F32),
            vmem((2, R, 2 * hid), BF16),
            vmem((2, R, hid), BF16),
            vmem((R, hid), BF16),
            vmem((2, R, hid), BF16),
            vmem((R, hid), BF16),
            vmem((hid, 2 * R), BF16),
            vmem((Y, X * C, 2 * R), BF16),
            dma((10,)),
            dma((4,)),
            dma((4,)),
            dma((4,)),
            dma((4, 2)),
            dma((6, 2 * H)),
            dma((6, 2 * H)),
            dma((7 + 2 * Y,)),
            dma((7,)),
            dma((4, 2 * H)),
            dma((4, 2 * H)),
        ],
        compiler_params=pltpu.CompilerParams(
            collective_id=0, has_side_effects=True, vmem_limit_bytes=63 * 1024 * 1024
        ),
    )(
        teacher_in,
        student_in,
        teacher_route.reshape(1, tokens),
        student_route.reshape(1, tokens),
        w1t[0],
        w2t[0],
        w1s[0],
        w2s[0],
    )
    return g1[None], g2[None]


def solution(mesh):
    return jax.shard_map(
        on_device,
        mesh=mesh,
        in_specs=(
            P("dp", None),
            P("dp", None),
            P("dp", None),
            P("dp", None),
            P("dp", None, "expert"),
            P("dp", "expert", None),
            P("dp", None, "expert"),
            P("dp", "expert", None),
        ),
        out_specs=(P("dp", None, "expert"), P("dp", "expert", None)),
        check_vma=False,
    )
```
